512 devices in a mesh: head: 8 (over x, core), tok: 64 (over z, y).
Axes of the slice: x: 4, y: 4, z: 16, core: 2. Of those that a mesh axis runs over, the one named last changes fastest.
Arguments:
- queries: bfloat16 [32768, 4096], P('tok', 'head'), may hold values from -16 to 16
- keys_fast: bfloat16 [32768, 4096], P('tok', 'head'), may hold values from -16 to 16
- values_fast: bfloat16 [32768, 4096], P('tok', 'head'), may hold values from -6 to 6
- keys_attn: bfloat16 [32768, 4096], P('tok', 'head'), may hold values from -16 to 16
- w_one: bfloat16 [8, 512, 256], P('head'), may hold values from -0.25 to 0.25
- w_three: bfloat16 [8, 512, 256], P('head'), may hold values from -0.25 to 0.25
- w_two: bfloat16 [8, 256, 512], P('head'), may hold values from -2 to 2
- step_size: float32 [8], P('head'), may hold values from 0.01 to 0.04
- norm_gain: float32 [4096], P('head'), may hold values from 0.25 to 1.75
- group_ids: int32 [32768], P('tok'), may hold values 0 or 1
- window_ids: int32 [32768], P('tok'), may hold values from 0 to 42, never falling along the last dimension, each value on 1 to 768 neighbouring positions
Outputs:
- mixed: bfloat16 [32768, 4096], P('tok', 'head')
The draws below stay inside these ranges and needn't reach their ends.
Inputs may be any that keep to these rules, and one draw needn't show every extreme that they name: `window_ids`: window numbers never fall along the sequence and each number occurs; a window has 1 to 768 tokens, one exactly 768.
All inputs are finite; a program needn't handle non-finite values. No bound on the sum of `group_ids` on one device may be relied on, other than what follows from the above.
Results may differ from the reference program's by a relative error of at most 0.013.
Values may be sent and summed in bfloat16 or wider, within the bound.
A program may use at most 64 MiB of HBM per device.

```python
import math
import jax
import jax.numpy as jnp
import numpy as np
from jax import lax

DH = 512
FW_HID = 256
HEADS = 8
WIN = 768
TOK_DEV = 512
TOKENS = 32768
NBACK = 3
NWIN = 43
N_TOK = 64


def draw_queries(key, part):
    key = jax.random.fold_in(key, 11)
    own_draw = jax.random.normal(key, (TOKENS, HEADS * DH), jnp.float32)
    return jnp.clip(own_draw, -16.0, 16.0).astype(jnp.bfloat16)


def draw_keys_attn(key, part):
    key = jax.random.fold_in(key, 12)
    own_draw = jax.random.normal(key, (TOKENS, HEADS * DH), jnp.float32)
    return jnp.clip(own_draw, -16.0, 16.0).astype(jnp.bfloat16)


def draw_keys_fast(key, part):
    key = jax.random.fold_in(key, 13)
    feature = (jnp.arange(HEADS * DH, dtype=jnp.int32) % DH).astype(jnp.float32) / (DH - 1)
    noise_key = jax.random.fold_in(key, 0)
    own_draw = jax.random.normal(noise_key, (TOKENS, HEADS * DH), jnp.float32)
    values = own_draw * (0.6 * jnp.exp(feature * math.log(3.0)))[None, :]
    return jnp.clip(values, -16.0, 16.0).astype(jnp.bfloat16)


def draw_w_two(key, part):
    key = jax.random.fold_in(key, 14)
    head_pos = jnp.arange(HEADS, dtype=jnp.float32)[:, None, None] / (HEADS - 1)
    own_draw = jax.random.normal(key, (HEADS, FW_HID, DH), jnp.float32)
    factor = 1.0 + 2.0 * head_pos
    return jnp.clip(own_draw * factor / math.sqrt(FW_HID), -2.0, 2.0).astype(jnp.bfloat16)


def plant(drawn, stream_key, low, top_value):
    place = [jax.random.randint(jax.random.fold_in(stream_key, axis), (), 0, length) for axis, length in enumerate(drawn.shape)]
    longest = drawn.shape.index(max(drawn.shape))
    beside = place[:longest] + [(place[longest] + 1) % drawn.shape[longest]] + place[longest + 1:]
    return drawn.at[tuple(place)].set(low).at[tuple(beside)].set(top_value)


def shard_levels(rng, dims, shards, smallest, high):
    factor_of, own = 1.0, jax.random.fold_in(rng, 6)
    for axis_at, blocks in shards:
        draws = jnp.exp(jax.random.uniform(jax.random.fold_in(own, axis_at), (blocks,), jnp.float32, smallest / len(shards), high / len(shards)))
        factor_of = factor_of * jnp.repeat(draws, dims[axis_at] // blocks).reshape([-1 if axis == axis_at else 1 for axis in range(len(dims))])
    return factor_of


def profile(amount, total, most, skew):
    weights = [(1 << 20) // math.isqrt(rank ** skew) + 1 for rank in range(2, amount + 1)]
    spare, given = total - most - (amount - 1), [1] * (amount - 1)
    while spare > 0:
        movable = [i for i in range(amount - 1) if given[i] < most]
        pool, left = sum([weights[i] for i in movable]), spare
        for i in movable:
            addition = min(most - given[i], max(1, left * weights[i] // pool), spare)
            given[i] = given[i] + addition
            spare = spare - addition
    return np.array([most] + given)


def ragged(stream_key, amount, total, most, skew):
    if amount == 2:
        one = jax.random.randint(stream_key, (), max(1, total - most), min(most, total - 1) + 1)
        return jnp.stack([one, total - one])
    lengths = jnp.asarray(profile(amount, total, most, skew), jnp.int32)
    couples = (amount - 1) // 2
    source_of, sink = lengths[1:1 + 2 * couples:2], lengths[2:2 + 2 * couples:2]
    room = jnp.minimum(source_of - 1, most - sink)
    shifted = jax.random.randint(jax.random.fold_in(stream_key, 1), (couples,), 0, 1 << 20) % (room + 1)
    lengths = lengths.at[1:1 + 2 * couples:2].set(source_of - shifted).at[2:2 + 2 * couples:2].set(sink + shifted)
    return lengths[jax.random.permutation(jax.random.fold_in(stream_key, 2), amount)]


def normal_values(rng, dims, width, most, pieces=(), kind=jnp.bfloat16):
    result = width * jax.random.normal(rng, dims, jnp.float32)
    if pieces:
        result = result * shard_levels(rng, dims, pieces, -0.22, 0.18)
    return jnp.clip(result, -most, most).astype(kind)


def setup_inputs(seed: int = 0) -> dict:
    key_list = jax.random.split(jax.random.key(seed), 12)
    queries = draw_queries(jax.random.fold_in(key_list[11], 71), 0)
    keys_fast = draw_keys_fast(jax.random.fold_in(key_list[11], 71), 0)
    values_fast = normal_values(key_list[2], (TOKENS, HEADS * DH), 1.0, 6.0, ((0, 64), (1, 8)))
    keys_attn = draw_keys_attn(jax.random.fold_in(key_list[11], 71), 0)
    w_one = normal_values(key_list[4], (HEADS, DH, FW_HID), DH ** -0.5, 0.25, ((0, 8),))
    w_three = normal_values(key_list[5], (HEADS, DH, FW_HID), DH ** -0.5, 0.25, ((0, 8),))
    w_two = draw_w_two(jax.random.fold_in(key_list[11], 71), 0)
    step_size = jnp.clip(jnp.exp(math.log(0.04) - 1.3862944 * jax.random.uniform(key_list[7], (HEADS,), jnp.float32) ** shard_levels(key_list[7], (HEADS,), ((0, 8),), -0.2, 0.2)), 0.01, 0.04)
    norm_gain = jnp.clip(1.0 + 0.15 * jax.random.normal(key_list[8], (HEADS * DH,), jnp.float32), 0.25, 1.75)
    group_ids = plant((jax.random.randint(key_list[9], (TOKENS,), 0, 2) < 1).astype(jnp.int32), jax.random.fold_in(key_list[9], 1), 0, 1)
    window_ids = jnp.searchsorted(jnp.cumsum(ragged(key_list[10], NWIN, TOKENS, WIN, 0)), jnp.arange(TOKENS), side="right").astype(jnp.int32)
    return dict(queries=queries, keys_fast=keys_fast, values_fast=values_fast, keys_attn=keys_attn, w_one=w_one, w_three=w_three, w_two=w_two, step_size=step_size, norm_gain=norm_gain, group_ids=group_ids, window_ids=window_ids)


EPSILON = 1e-06

def fast_grads(keys_rows, value_rows, group_mask, w_one, w_three, w_two):
    pre_one = jnp.dot(keys_rows, w_one, preferred_element_type=jnp.float32)
    pre_three = jnp.dot(keys_rows, w_three, preferred_element_type=jnp.float32)
    sigmoid_one = jax.nn.sigmoid(pre_one)
    hidden_act = (pre_one * sigmoid_one * pre_three * group_mask).astype(jnp.bfloat16)
    back_grad = jnp.dot(value_rows, w_two.T, preferred_element_type=jnp.float32)
    delta_one = (-back_grad * pre_three * sigmoid_one * (1.0 + pre_one * (1.0 - sigmoid_one)) * group_mask).astype(jnp.bfloat16)
    delta_three = (-back_grad * pre_one * sigmoid_one * group_mask).astype(jnp.bfloat16)
    grad_one = jnp.dot(keys_rows.T, delta_one, preferred_element_type=jnp.float32)
    grad_three = jnp.dot(keys_rows.T, delta_three, preferred_element_type=jnp.float32)
    grad_two = -jnp.dot(hidden_act.T, value_rows, preferred_element_type=jnp.float32)
    return (grad_one, grad_three, grad_two)

def normalized_step(weight, grad, rate):
    mean_sq = jnp.mean(grad * grad)
    return (weight.astype(jnp.float32) - rate * grad * lax.rsqrt(mean_sq + EPSILON)).astype(jnp.bfloat16)

def fast_apply(query_rows, w_one, w_three, w_two):
    pre_one = jnp.dot(query_rows, w_one, preferred_element_type=jnp.float32)
    pre_three = jnp.dot(query_rows, w_three, preferred_element_type=jnp.float32)
    hidden_act = (pre_one * jax.nn.sigmoid(pre_one) * pre_three).astype(jnp.bfloat16)
    return jnp.dot(hidden_act, w_two, preferred_element_type=jnp.float32)

def reference(queries, keys_fast, values_fast, keys_attn, w_one, w_three, w_two, step_size, norm_gain, group_ids, window_ids):

    def by_heads(array):
        return jnp.transpose(array.reshape(TOKENS, HEADS, DH), (1, 0, 2))
    in_first = (group_ids == 0).astype(jnp.float32)[:, None]
    in_second = 1.0 - in_first

    def head_pass(packed):
        query_rows, keys_rows, value_rows, weight_one, weight_three, weight_two, rate = packed
        outputs = []
        for group_mask in (in_first, in_second):
            grad_one, grad_three, grad_two = fast_grads(keys_rows, value_rows, group_mask, weight_one, weight_three, weight_two)
            weight_one = normalized_step(weight_one, grad_one, rate)
            weight_three = normalized_step(weight_three, grad_three, rate)
            weight_two = normalized_step(weight_two, grad_two, rate)
            outputs.append(fast_apply(query_rows, weight_one, weight_three, weight_two))
        return jnp.where(in_first > 0.5, outputs[0], outputs[1])
    fast = lax.map(head_pass, (by_heads(queries), by_heads(keys_fast), by_heads(values_fast), w_one, w_three, w_two, step_size))
    sum_sq = lax.optimization_barrier(jnp.sum(fast * fast, axis=(0, 2)))
    inverse = lax.rsqrt(sum_sq / (HEADS * DH) + EPSILON)
    values = (fast * inverse[None, :, None] * norm_gain.reshape(HEADS, 1, DH)).astype(jnp.bfloat16)
    reach = NBACK * TOK_DEV
    score_scale = 1.0 / math.sqrt(DH)
    padded_windows = jnp.concatenate([jnp.full((reach,), -4, jnp.int32), window_ids.astype(jnp.int32)])

    def attend_head(packed):
        query_rows, key_rows, value_rows = packed
        padded_keys = jnp.concatenate([jnp.zeros((reach, DH), jnp.bfloat16), key_rows])
        padded_values = jnp.concatenate([jnp.zeros((reach, DH), jnp.bfloat16), value_rows])

        def query_block(block_start):
            query_part = lax.dynamic_slice_in_dim(query_rows, block_start, TOK_DEV, 0)
            key_part = lax.dynamic_slice_in_dim(padded_keys, block_start, reach + TOK_DEV, 0)
            value_part = lax.dynamic_slice_in_dim(padded_values, block_start, reach + TOK_DEV, 0)
            query_window = lax.dynamic_slice_in_dim(window_ids.astype(jnp.int32), block_start, TOK_DEV, 0)
            key_window = lax.dynamic_slice_in_dim(padded_windows, block_start, reach + TOK_DEV, 0)
            query_pos = block_start + jnp.arange(TOK_DEV, dtype=jnp.int32)
            key_pos = block_start - reach + jnp.arange(reach + TOK_DEV, dtype=jnp.int32)
            allowed = (key_pos[None, :] <= query_pos[:, None]) & (key_pos[None, :] >= 0) & (key_window[None, :] >= query_window[:, None] - 1)
            scores = jnp.dot(query_part, key_part.T, preferred_element_type=jnp.float32) * score_scale
            scores = jnp.where(allowed, scores, -1e+30)
            row_max = lax.optimization_barrier(jnp.max(scores, axis=1, keepdims=True))
            expo = jnp.where(allowed, jnp.exp(scores - row_max), 0.0)
            probs = (expo / lax.optimization_barrier(jnp.sum(expo, axis=1, keepdims=True))).astype(jnp.bfloat16)
            return jnp.dot(probs, value_part, preferred_element_type=jnp.float32).astype(jnp.bfloat16)
        starts = jnp.arange(N_TOK, dtype=jnp.int32) * TOK_DEV
        return lax.map(query_block, starts).reshape(TOKENS, DH)
    mixed = lax.map(attend_head, (by_heads(queries), by_heads(keys_attn), values))
    return jnp.transpose(mixed, (1, 0, 2)).reshape(TOKENS, HEADS * DH)
```

```python
import functools
import math

import jax
import jax.numpy as jnp
from jax import lax
from jax.experimental import pallas as pl
from jax.experimental.pallas import tpu as pltpu
from jax.sharding import PartitionSpec as P

NY = 4
NCORE = 2
NBACK = 3
EPSILON = 1e-06
MESH = pl.DeviceIdType.MESH
F32 = jnp.float32
BF16 = jnp.bfloat16


def dot_nt(a, b):
    return lax.dot_general(a, b, (((1,), (1,)), ((), ())), preferred_element_type=F32)


def dot_nn(a, b):
    return lax.dot_general(a, b, (((1,), (0,)), ((), ())), preferred_element_type=F32)


def sigmoid(x):
    return 0.5 * jnp.tanh(0.5 * x) + 0.5


def aligned(index, step):
    return pl.ds(pl.multiple_of(index * step, step), step)


def kernel(
    dims,
    k_ref,
    v_ref,
    w1_ref,
    w3_ref,
    w2_ref,
    rate_ref,
    gain_ref,
    gid_ref,
    wid_ref,
    q_hbm,
    a_hbm,
    out_ref,
    qall,
    aall,
    ids,
    pre,
    back,
    delta,
    grad_send,
    grad_own,
    y_in,
    z_out,
    z_own,
    z_in,
    gathered,
    weights,
    w2t,
    scores,
    probs,
    hidden,
    fast,
    values,
    sq_in,
    local_sem,
    y_send,
    y_recv,
    z_send,
    z_recv,
    zg_send,
    zg_recv,
    yg_send,
    yg_recv,
    halo_send,
    halo_recv,
    head_send,
    head_recv,
):
    nz, nhead, rows, dh, hid = dims
    ntok = nz * NY
    cols = dh // 128
    head_rows = 2 * hid // NY
    tail_rows = hid // NY
    piece = head_rows + tail_rows
    block = piece * cols // nz
    t = lax.axis_index("tok")
    h = lax.axis_index("head")
    z = lax.div(t, NY)
    y = lax.rem(t, NY)

    def y_peer(d):
        return z * NY + lax.rem(y + d, NY)

    def z_peer(d):
        return lax.rem(z + d, nz) * NY + y

    def remote(src, dst, send, recv, **where):
        return pltpu.make_async_remote_copy(
            src_ref=src, dst_ref=dst, send_sem=send, recv_sem=recv, device_id=where, device_id_type=MESH
        )

    load_a = pltpu.make_async_copy(a_hbm, aall.at[NBACK], local_sem.at[0])
    load_q = pltpu.make_async_copy(q_hbm, qall.at[NBACK], local_sem.at[1])
    load_a.start()
    load_q.start()

    barrier = pltpu.get_barrier_semaphore()

    def greet(**where):
        pl.semaphore_signal(barrier, inc=1, device_id=where, device_id_type=MESH)

    for d in range(1, NY):
        greet(tok=y_peer(d))

    @pl.loop(1, nz)
    def _(d):
        greet(tok=z_peer(d))

    for d in range(1, NBACK + 1):
        greet(tok=lax.rem(t + ntok - d, ntok))
    for d in range(1, nhead):
        greet(head=lax.rem(h + d, nhead))

    ids[NBACK, 0:1, :] = wid_ref[...].reshape(1, rows)
    ids[NBACK, 1:2, :] = gid_ref[...].reshape(1, rows)
    weights[0, 0:hid, :] = w1_ref[0].T
    weights[0, hid : 2 * hid, :] = w3_ref[0].T
    weights[0, 2 * hid : 3 * hid, :] = w2_ref[0]

    def y_scatter(r, d):
        p = lax.rem(y + d, NY)
        return remote(
            grad_send.at[r, p], y_in.at[r, d - 1], y_send.at[r, d - 1], y_recv.at[r, d - 1], tok=y_peer(d)
        )

    def z_scatter(r, d):
        n = lax.rem(z + d, nz)
        return remote(
            z_out.at[r, aligned(n, block)],
            z_in.at[r, d - 1],
            z_send.at[r, d - 1],
            z_recv.at[r, d - 1],
            tok=z_peer(d),
        )

    def z_gather(r, d, owner):
        part = gathered.at[r, y, aligned(owner, block)]
        return remote(part, part, zg_send.at[r, d - 1], zg_recv.at[r, d - 1], tok=z_peer(d))

    def y_gather(r, d, owner):
        part = gathered.at[r, owner]
        return remote(part, part, yg_send.at[r, d - 1], yg_recv.at[r, d - 1], tok=y_peer(d))

    def halo(which, d):
        buffer = (aall, qall, ids)[which]
        return remote(
            buffer.at[NBACK],
            buffer.at[NBACK - d],
            halo_send.at[which, d - 1],
            halo_recv.at[which, d - 1],
            tok=lax.rem(t + d, ntok),
        )

    def head_share(d):
        return remote(
            sq_in.at[0], sq_in.at[d], head_send.at[d - 1], head_recv.at[d - 1], head=lax.rem(h + d, nhead)
        )

    def gradients(r):
        pre[...] = dot_nt(weights[r, 0 : 2 * hid, :], k_ref[...])
        back[0:hid, :] = dot_nt(weights[r, 2 * hid : 3 * hid, :], v_ref[...])
        mask = (ids[NBACK, 1:2, :] == r).astype(F32)

        @pl.loop(0, hid // 32)
        def _(i):
            p1 = pre[aligned(i, 32), :]
            p3 = pre[pl.ds(pl.multiple_of(hid + i * 32, 32), 32), :]
            b = back[aligned(i, 32), :] * mask
            s1 = sigmoid(p1)
            silu = p1 * s1
            delta[aligned(i, 32), :] = (-b * p3 * s1 * (1.0 + p1 * (1.0 - s1))).astype(BF16)
            delta[pl.ds(pl.multiple_of(hid + i * 32, 32), 32), :] = (-b * silu).astype(BF16)
            delta[pl.ds(pl.multiple_of(2 * hid + i * 32, 32), 32), :] = (-silu * p3 * mask).astype(BF16)

        for d in (1, 2, 3, 0):
            p = lax.rem(y + d, NY)
            upper = dot_nn(delta[aligned(p, head_rows), :], k_ref[...])
            lower = dot_nn(
                delta[pl.ds(pl.multiple_of(2 * hid + p * tail_rows, tail_rows), tail_rows), :], v_ref[...]
            )
            for j in range(cols):
                top = slice(j * piece, j * piece + head_rows)
                bottom = slice(j * piece + head_rows, (j + 1) * piece)
                lanes = slice(j * 128, (j + 1) * 128)
                if d:
                    grad_send[r, p, top, :] = upper[:, lanes].astype(BF16)
                    grad_send[r, p, bottom, :] = lower[:, lanes].astype(BF16)
                else:
                    grad_own[top, :] = upper[:, lanes]
                    grad_own[bottom, :] = lower[:, lanes]
            if d:
                if r == 0 and d == 1:
                    pl.semaphore_wait(barrier, (NY - 1) + (nz - 1) + NBACK + (nhead - 1))
                y_scatter(r, d).start()

    def scatter_z(r):
        for d in range(1, NY):
            y_scatter(r, d).wait_recv()

        def total(n):
            own = grad_own[aligned(n, block), :]
            for d in range(1, NY):
                own = own + y_in[r, d - 1, aligned(n, block), :].astype(F32)
            return own

        @pl.loop(1, nz)
        def _(d):
            n = lax.rem(z + d, nz)
            z_out[r, aligned(n, block), :] = total(n).astype(BF16)
            z_scatter(r, d).start()

        z_own[...] = total(z)

    def gather_z(r):
        def add(d, total):
            z_scatter(r, d).wait_recv()
            return total + z_in[r, d - 1].astype(F32)

        total = lax.fori_loop(1, nz, add, z_own[...])
        gathered[r, y, aligned(z, block), :] = total.astype(BF16)

        @pl.loop(1, nz)
        def _(d):
            z_gather(r, d, z).start()

    def gather_y(r):
        @pl.loop(1, nz)
        def _(d):
            z_gather(r, d, lax.rem(z + nz - d, nz)).wait_recv()

        for d in range(1, NY):
            y_gather(r, d, y).start()

    def finish_y(r):
        for d in range(1, NY):
            y_gather(r, d, lax.rem(y + NY - d, NY)).wait_recv()

    def update(r):
        def squares(x):
            x = x.astype(F32)
            return jnp.sum((x * x).reshape(-1, 8, 128), axis=0)

        sums = [jnp.zeros((8, 128), F32) for _ in range(3)]
        for p in range(NY):
            for j in range(cols):
                which = p // (NY // 2)
                sums[which] = sums[which] + squares(gathered[r, p, j * piece : j * piece + head_rows, :])
                sums[2] = sums[2] + squares(gathered[r, p, j * piece + head_rows : (j + 1) * piece, :])
        scale = [
            rate_ref[...] * lax.rsqrt(jnp.sum(s, axis=(0, 1), keepdims=True) / float(hid * dh) + EPSILON)
            for s in sums
        ]
        for p in range(NY):
            for j in range(cols):
                lanes = slice(j * 128, (j + 1) * 128)
                top = slice(p * head_rows, (p + 1) * head_rows)
                bottom = slice(2 * hid + p * tail_rows, 2 * hid + (p + 1) * tail_rows)
                upper = gathered[r, p, j * piece : j * piece + head_rows, :].astype(F32)
                lower = gathered[r, p, j * piece + head_rows : (j + 1) * piece, :].astype(F32)
                weights[r + 1, top, lanes] = (
                    weights[r, top, lanes].astype(F32) - upper * scale[p // (NY // 2)]
                ).astype(BF16)
                weights[r + 1, bottom, lanes] = (
                    weights[r, bottom, lanes].astype(F32) - lower * scale[2]
                ).astype(BF16)

    def attend():
        for which in (0, 2):
            for d in range(1, NBACK + 1):
                halo(which, d).wait_recv()

        @pl.loop(0, NBACK + 1)
        def _(s):
            scores[s] = dot_nt(qall[NBACK], aall[s])

        mark = jnp.broadcast_to(ids[NBACK, 0:1, :].astype(F32), (128, rows)).T
        back[0:rows, 0:128] = mark

        @pl.loop(0, rows // 16)
        def _(i):
            here = aligned(i, 16)
            query_mark = back[here, 0:1] - 1.0
            query_at = t * rows + i * 16 + lax.broadcasted_iota(jnp.int32, (16, rows), 0)
            parts = []
            for s in range(NBACK + 1):
                key_at = (t - NBACK + s) * rows + lax.broadcasted_iota(jnp.int32, (16, rows), 1)
                allowed = (
                    (key_at <= query_at) & (key_at >= 0) & (ids[s, 0:1, :].astype(F32) >= query_mark)
                )
                parts.append(jnp.where(allowed, scores[s, here, :] * (1.0 / math.sqrt(dh)), -1e30))
            top = parts[0]
            for part in parts[1:]:
                top = jnp.maximum(top, part)
            top = jnp.max(top, axis=1, keepdims=True)
            parts = [jnp.exp(part - top) for part in parts]
            whole = parts[0]
            for part in parts[1:]:
                whole = whole + part
            inverse = 1.0 / jnp.sum(whole, axis=1, keepdims=True)
            for s in range(NBACK + 1):
                probs[s, here, :] = (parts[s] * inverse).astype(BF16)

    def apply_fast(r):
        w2t[...] = weights[r + 1, 2 * hid : 3 * hid, :].T

        @pl.loop(0, NBACK + 1)
        def _(s):
            pre[...] = dot_nt(weights[r + 1, 0 : 2 * hid, :], qall[s])

            @pl.loop(0, hid // 32)
            def _(i):
                p1 = pre[aligned(i, 32), :]
                p3 = pre[pl.ds(pl.multiple_of(hid + i * 32, 32), 32), :]
                hidden[aligned(i, 32), :] = (p1 * sigmoid(p1) * p3).astype(BF16)

            if r == 0:
                fast[s] = dot_nn(w2t[...], hidden[...])
            else:
                pre[...] = dot_nn(w2t[...], hidden[...])
                first = ids[s, 1:2, :] == 0

                def select(i, total):
                    here = aligned(i, 32)
                    mixed = jnp.where(first, fast[s, here, :], pre[here, :])
                    fast[s, here, :] = mixed
                    return total + jnp.sum((mixed * mixed).reshape(4, 8, rows), axis=0)

                total = lax.fori_loop(0, dh // 32, select, jnp.zeros((8, rows), F32))
                total = jnp.sum(total, axis=0, keepdims=True)
                for j in range(rows // 128):
                    sq_in[0, s, j : j + 1, :] = total[:, j * 128 : (j + 1) * 128]

    gradients(0)
    scatter_z(0)
    load_a.wait()
    for d in range(1, NBACK + 1):
        halo(2, d).start()
        halo(0, d).start()
    gather_z(0)
    gather_y(0)
    load_q.wait()
    finish_y(0)
    update(0)
    gradients(1)
    scatter_z(1)
    for d in range(1, NBACK + 1):
        halo(1, d).start()
    attend()
    gather_z(1)
    gather_y(1)
    for d in range(1, NBACK + 1):
        halo(1, d).wait_recv()
    apply_fast(0)
    finish_y(1)
    update(1)
    apply_fast(1)
    for d in range(1, nhead):
        head_share(d).start()
    for d in range(1, nhead):
        head_share(d).wait_recv()

    for s in range(NBACK + 1):
        total = sq_in[0, s]
        for d in range(1, nhead):
            total = total + sq_in[d, s]
        inverse = lax.rsqrt(total / float(nhead * dh) + EPSILON)
        inverse = jnp.concatenate([inverse[j : j + 1, :] for j in range(rows // 128)], axis=1)

        @pl.loop(0, dh // 32)
        def _(i):
            here = aligned(i, 32)
            values[here, s * rows : (s + 1) * rows] = (fast[s, here, :] * inverse).astype(BF16)

    for s in range(NBACK + 1):
        product = dot_nt(probs[s], values[:, s * rows : (s + 1) * rows])
        pre[...] = product if s == 0 else pre[...] + product
    out_ref[...] = (pre[...] * gain_ref[...].reshape(1, dh)).astype(BF16)

    for r in range(2):
        for d in range(1, NY):
            y_scatter(r, d).wait_send()
            y_gather(r, d, y).wait_send()

        @pl.loop(1, nz)
        def _(d):
            z_scatter(r, d).wait_send()
            z_gather(r, d, z).wait_send()

    for which in range(3):
        for d in range(1, NBACK + 1):
            halo(which, d).wait_send()
    for d in range(1, nhead):
        head_share(d).wait_send()


def shards(queries, keys_fast, values_fast, keys_attn, w_one, w_three, w_two, step_size, norm_gain, group_ids, window_ids):
    rows, dh = queries.shape
    hid = w_one.shape[2]
    nz = lax.axis_size("tok") // NY
    nhead = lax.axis_size("head")
    piece = 3 * hid // NY * (dh // 128)
    block = piece // nz
    dma = pltpu.SemaphoreType.DMA
    vmem = pl.BlockSpec(memory_space=pltpu.VMEM)
    anywhere = pl.BlockSpec(memory_space=pl.ANY)
    return pl.pallas_call(
        functools.partial(kernel, (nz, nhead, rows, dh, hid)),
        out_shape=jax.ShapeDtypeStruct((rows, dh), BF16),
        in_specs=[vmem] * 9 + [anywhere] * 2,
        out_specs=vmem,
        scratch_shapes=[
            pltpu.VMEM((NBACK + 1, rows, dh), BF16),
            pltpu.VMEM((NBACK + 1, rows, dh), BF16),
            pltpu.VMEM((NBACK + 1, 8, rows), jnp.int32),
            pltpu.VMEM((2 * hid, rows), F32),
            pltpu.VMEM((max(hid, rows), rows), F32),
            pltpu.VMEM((3 * hid, rows), BF16),
            pltpu.VMEM((2, NY, piece, 128), BF16),
            pltpu.VMEM((piece, 128), F32),
            pltpu.VMEM((2, NY - 1, piece, 128), BF16),
            pltpu.VMEM((2, piece, 128), BF16),
            pltpu.VMEM((block, 128), F32),
            pltpu.VMEM((2, nz - 1, block, 128), BF16),
            pltpu.VMEM((2, NY, piece, 128), BF16),
            pltpu.VMEM((3, 3 * hid, dh), BF16),
            pltpu.VMEM((dh, hid), BF16),
            pltpu.VMEM((NBACK + 1, rows, rows), F32),
            pltpu.VMEM((NBACK + 1, rows, rows), BF16),
            pltpu.VMEM((hid, rows), BF16),
            pltpu.VMEM((NBACK + 1, dh, rows), F32),
            pltpu.VMEM((dh, (NBACK + 1) * rows), BF16),
            pltpu.VMEM((nhead, NBACK + 1, rows // 128, 128), F32),
            dma((2,)),
            dma((2, NY - 1)),
            dma((2, NY - 1)),
            dma((2, nz - 1)),
            dma((2, nz - 1)),
            dma((2, nz - 1)),
            dma((2, nz - 1)),
            dma((2, NY - 1)),
            dma((2, NY - 1)),
            dma((3, NBACK)),
            dma((3, NBACK)),
            dma((nhead - 1,)),
            dma((nhead - 1,)),
        ],
        compiler_params=pltpu.CompilerParams(
            collective_id=0, has_side_effects=True, vmem_limit_bytes=56 * 1024 * 1024
        ),
        name="fast_weight_attention",
    )(
        keys_fast,
        values_fast,
        w_one,
        w_three,
        w_two,
        step_size.reshape(1, 1),
        norm_gain,
        group_ids,
        window_ids,
        queries,
        keys_attn,
    )


def solution(mesh):
    in_specs = (
        P("tok", "head"),
        P("tok", "head"),
        P("tok", "head"),
        P("tok", "head"),
        P("head", None, None),
        P("head", None, None),
        P("head", None, None),
        P("head"),
        P("head"),
        P("tok"),
        P("tok"),
    )
    return jax.shard_map(shards, mesh=mesh, in_specs=in_specs, out_specs=P("tok", "head"), check_vma=False)
```

```python
import functools
import math

import jax
import jax.numpy as jnp
from jax import lax
from jax.experimental import pallas as pl
from jax.experimental.pallas import tpu as pltpu
from jax.sharding import PartitionSpec as P

NY = 4
NCORE = 2
NBACK = 3
KEY_PARTS = 8
EPSILON = 1e-06
MESH = pl.DeviceIdType.MESH
F32 = jnp.float32
BF16 = jnp.bfloat16


def dot_nt(a, b):
    return lax.dot_general(a, b, (((1,), (1,)), ((), ())), preferred_element_type=F32)


def dot_nn(a, b):
    return lax.dot_general(a, b, (((1,), (0,)), ((), ())), preferred_element_type=F32)


def sigmoid(x):
    return 0.5 * jnp.tanh(0.5 * x) + 0.5


def aligned(index, step):
    return pl.ds(pl.multiple_of(index * step, step), step)


def kernel(
    dims,
    k_ref,
    v_ref,
    w1_ref,
    w3_ref,
    w2_ref,
    rate_ref,
    gain_ref,
    gid_ref,
    wid_ref,
    q_ref,
    a_hbm,
    out_ref,
    aall,
    ids,
    pre,
    back,
    delta,
    weights,
    w2t,
    scores,
    probs,
    hidden_first,
    hidden,
    fast,
    norms,
    sq_in,
    local_sem,
    halo_sems,
    head_sems,
    key_sems,
    *chunks,
):
    nz, nhead, rows, dh, hid = dims
    ntok = nz * NY
    cols = dh // 128
    t = lax.axis_index("tok")
    h = lax.axis_index("head")
    z = lax.div(t, NY)
    y = lax.rem(t, NY)
    starts = (0, 2 * hid)
    heights = (2 * hid // NY, hid // NY)
    pieces = tuple(height * cols for height in heights)
    blocks = tuple(piece // nz for piece in pieces)

    def y_peer(d):
        return z * NY + lax.rem(y + d, NY)

    def z_peer(d):
        return lax.rem(z + d, nz) * NY + y

    def remote(src, dst, sems, index, **where):
        return pltpu.make_async_remote_copy(
            src_ref=src,
            dst_ref=dst,
            send_sem=sems.at[(0, *index)],
            recv_sem=sems.at[(1, *index)],
            device_id=where,
            device_id_type=MESH,
        )

    load_a = pltpu.make_async_copy(a_hbm, aall.at[NBACK], local_sem)
    load_a.start()

    barrier = pltpu.get_barrier_semaphore()

    def greet(**where):
        pl.semaphore_signal(barrier, inc=1, device_id=where, device_id_type=MESH)

    @pl.loop(1, nz)
    def _(d):
        greet(tok=z_peer(d))

    for d in range(1, NY):
        greet(tok=y_peer(d))
    for d in range(1, NBACK + 1):
        greet(tok=lax.rem(t + ntok - d, ntok))
    for d in range(1, nhead):
        greet(head=lax.rem(h + d, nhead))

    ids[NBACK, 0:1, :] = wid_ref[...].reshape(1, rows)
    ids[NBACK, 1:2, :] = gid_ref[...].reshape(1, rows)
    weights[0, 0:hid, :] = w1_ref[0].T
    weights[0, hid : 2 * hid, :] = w3_ref[0].T
    weights[0, 2 * hid : 3 * hid, :] = w2_ref[0]

    def y_scatter(r, c, d):
        grad_send, y_in, sems = chunks[c][0], chunks[c][1], chunks[c][7]
        return remote(
            grad_send.at[r, lax.rem(y + d, NY)], y_in.at[r, d - 1], sems, (r, d - 1), tok=y_peer(d)
        )

    def z_scatter(r, c, d):
        z_out, z_in, sems = chunks[c][3], chunks[c][5], chunks[c][8]
        n = lax.rem(z + d, nz)
        return remote(
            z_out.at[r, aligned(n, blocks[c])], z_in.at[r, d - 1], sems, (r, d - 1), tok=z_peer(d)
        )

    def z_gather(r, c, d, owner):
        part = chunks[c][6].at[r, y, aligned(owner, blocks[c])]
        return remote(part, part, chunks[c][9], (r, d - 1), tok=z_peer(d))

    def y_gather(r, c, d, owner):
        part = chunks[c][6].at[r, owner]
        return remote(part, part, chunks[c][10], (r, d - 1), tok=y_peer(d))

    def key_piece(n):
        d = (1, 3, 2)[n % NBACK]
        part = n // NBACK
        here = slice(part * rows // KEY_PARTS, (part + 1) * rows // KEY_PARTS)
        return remote(
            aall.at[NBACK, here],
            aall.at[NBACK - d, here],
            key_sems,
            (d - 1, part),
            tok=lax.rem(t + d, ntok),
        )

    def reaches(shard, n):
        left = lax.rem(shard, 3)
        return left != 0 if n // NBACK >= KEY_PARTS // 2 else left == 1

    def send_keys(first, last):
        for n in range(first, last):
            if n % NBACK == 1:

                @pl.when(reaches(lax.rem(t + NBACK, ntok), n))
                def _():
                    key_piece(n).start()
            else:
                key_piece(n).start()

    def wait_keys(sent):
        for n in range(NBACK * KEY_PARTS):
            wait = key_piece(n).wait_send if sent else key_piece(n).wait_recv
            if n % NBACK == 1:
                pl.when(reaches(lax.rem(t + NBACK, ntok) if sent else t, n))(wait)
            else:
                wait()

    def halo(which, d):
        buffer = (ids, hidden, norms)[which]
        return remote(
            buffer.at[NBACK], buffer.at[NBACK - d], halo_sems, (which, d - 1), tok=lax.rem(t + d, ntok)
        )

    def head_share(d):
        return remote(sq_in.at[0], sq_in.at[d], head_sems, (d - 1,), head=lax.rem(h + d, nhead))

    def send_halo(which, *distances):
        for d in distances:
            halo(which, d).start()

    def swiglu(i):
        p1 = pre[aligned(i, 32), :]
        p3 = pre[pl.ds(pl.multiple_of(hid + i * 32, 32), 32), :]
        return p1 * sigmoid(p1) * p3

    def gradients(r):
        pre[...] = dot_nt(weights[r, 0 : 2 * hid, :], k_ref[...])
        back[0:hid, :] = dot_nt(weights[r, 2 * hid : 3 * hid, :], v_ref[...])
        mask = (ids[NBACK, 1:2, :] == r).astype(F32)

        @pl.loop(0, hid // 32)
        def _(i):
            p1 = pre[aligned(i, 32), :]
            p3 = pre[pl.ds(pl.multiple_of(hid + i * 32, 32), 32), :]
            b = back[aligned(i, 32), :] * mask
            s1 = sigmoid(p1)
            silu = p1 * s1
            delta[aligned(i, 32), :] = (-b * p3 * s1 * (1.0 + p1 * (1.0 - s1))).astype(BF16)
            delta[pl.ds(pl.multiple_of(hid + i * 32, 32), 32), :] = (-b * silu).astype(BF16)
            delta[pl.ds(pl.multiple_of(2 * hid + i * 32, 32), 32), :] = (-silu * p3 * mask).astype(BF16)

        if r == 0:
            pl.semaphore_wait(barrier, (NY - 1) + (nz - 1) + NBACK + (nhead - 1))
        for c in range(2):
            grad_send, grad_own = chunks[c][0], chunks[c][2]
            height = heights[c]
            for d in (1, 3, 2, 0):
                p = lax.rem(y + d, NY)
                here = pl.ds(pl.multiple_of(starts[c] + p * height, height), height)
                grad = dot_nn(delta[here, :], (k_ref, v_ref)[c][...])
                for j in range(cols):
                    part = grad[:, j * 128 : (j + 1) * 128]
                    if d:
                        grad_send[r, p, j * height : (j + 1) * height, :] = part.astype(BF16)
                    else:
                        grad_own[j * height : (j + 1) * height, :] = part
                if d:
                    y_scatter(r, c, d).start()

    def scatter_z(r, c):
        y_in, grad_own, z_out, z_own = chunks[c][1:5]
        for d in range(1, NY):
            y_scatter(r, c, d).wait_recv()

        def total(n):
            own = grad_own[aligned(n, blocks[c]), :]
            for d in range(1, NY):
                own = own + y_in[r, d - 1, aligned(n, blocks[c]), :].astype(F32)
            return own

        @pl.loop(1, nz)
        def _(d):
            z_out[r, aligned(lax.rem(z + d, nz), blocks[c]), :] = total(lax.rem(z + d, nz)).astype(BF16)
            z_scatter(r, c, d).start()

        z_own[...] = total(z)

    def gather_z(r, c):
        z_own, z_in, gathered = chunks[c][4:7]

        def add(d, total):
            z_scatter(r, c, d).wait_recv()
            return total + z_in[r, d - 1].astype(F32)

        total = lax.fori_loop(1, nz, add, z_own[...])
        gathered[r, y, aligned(z, blocks[c]), :] = total.astype(BF16)

        @pl.loop(1, nz)
        def _(d):
            z_gather(r, c, d, z).start()

    def gather_y(r, c):
        @pl.loop(1, nz)
        def _(d):
            z_gather(r, c, d, lax.rem(z + nz - d, nz)).wait_recv()

        for d in (1, 3, 2):
            y_gather(r, c, d, y).start()

    def finish_y(r, c):
        for d in range(1, NY):
            y_gather(r, c, d, lax.rem(y + NY - d, NY)).wait_recv()

    def step_scale(r, c, owners):
        gathered = chunks[c][6]
        total = jnp.zeros((8, 128), F32)
        for p in owners:
            for j in range(cols):
                x = gathered[r, p, j * heights[c] : (j + 1) * heights[c], :].astype(F32)
                total = total + jnp.sum((x * x).reshape(-1, 8, 128), axis=0)
        mean = jnp.sum(total, axis=(0, 1), keepdims=True) / float(hid * dh)
        return rate_ref[...] * lax.rsqrt(mean + EPSILON)

    def update(r, c):
        gathered = chunks[c][6]
        height = heights[c]
        parts = ((0, 1), (2, 3)) if c == 0 else ((0, 1, 2, 3),)
        for owners in parts:
            scale = step_scale(r, c, owners)
            for p in owners:
                for j in range(cols):
                    here = slice(starts[c] + p * height, starts[c] + (p + 1) * height)
                    lanes = slice(j * 128, (j + 1) * 128)
                    grad = gathered[r, p, j * height : (j + 1) * height, :].astype(F32)
                    weights[r + 1, here, lanes] = (
                        weights[r, here, lanes].astype(F32) - grad * scale
                    ).astype(BF16)

    def attend():
        wait_keys(False)

        @pl.loop(0, NBACK + 1)
        def _(s):
            scores[s] = dot_nt(q_ref[...], aall[s])

        mark = jnp.broadcast_to(ids[NBACK, 0:1, :].astype(F32), (128, rows)).T
        back[0:rows, 0:128] = mark

        @pl.loop(0, rows // 16)
        def _(i):
            here = aligned(i, 16)
            query_mark = back[here, 0:1] - 1.0
            query_at = t * rows + i * 16 + lax.broadcasted_iota(jnp.int32, (16, rows), 0)
            parts = []
            for s in range(NBACK + 1):
                key_at = (t - NBACK + s) * rows + lax.broadcasted_iota(jnp.int32, (16, rows), 1)
                allowed = (
                    (key_at <= query_at) & (key_at >= 0) & (ids[s, 0:1, :].astype(F32) >= query_mark)
                )
                parts.append(jnp.where(allowed, scores[s, here, :] * (1.0 / math.sqrt(dh)), -1e30))
            top = parts[0]
            for part in parts[1:]:
                top = jnp.maximum(top, part)
            top = jnp.max(top, axis=1, keepdims=True)
            parts = [jnp.exp(part - top) for part in parts]
            whole = parts[0]
            for part in parts[1:]:
                whole = whole + part
            inverse = 1.0 / jnp.sum(whole, axis=1, keepdims=True)
            for s in range(NBACK + 1):
                probs[s, here, :] = (parts[s] * inverse).astype(BF16)

    def apply_first():
        w2t[0] = weights[1, 2 * hid : 3 * hid, :].T
        pre[...] = dot_nt(weights[1, 0 : 2 * hid, :], q_ref[...])

        @pl.loop(0, hid // 32)
        def _(i):
            hidden_first[aligned(i, 32), :] = swiglu(i).astype(BF16)

    def apply_second():
        pre[...] = dot_nt(weights[2, 0 : 2 * hid, :], q_ref[...])
        first = ids[NBACK, 1:2, :] == 0

        @pl.loop(0, hid // 32)
        def _(i):
            here = aligned(i, 32)
            own = hidden_first[here, :].astype(F32)
            hidden[NBACK, here, :] = jnp.where(first, own, swiglu(i)).astype(BF16)

    def project(s):
        fast[...] = dot_nn(w2t[0], hidden[s])
        pre[...] = dot_nn(w2t[1], hidden[s])

    def mixed_rows(s, i):
        here = aligned(i, 32)
        return jnp.where(ids[s, 1:2, :] == 0, fast[here, :], pre[here, :])

    def share_norm():
        def add(i, total):
            x = mixed_rows(NBACK, i)
            return total + jnp.sum((x * x).reshape(4, 8, rows), axis=0)

        total = lax.fori_loop(0, dh // 32, add, jnp.zeros((8, rows), F32))
        total = jnp.sum(total, axis=0, keepdims=True)
        for j in range(rows // 128):
            sq_in[0, j : j + 1, :] = total[:, j * 128 : (j + 1) * 128]
        for d in range(1, nhead):
            head_share(d).start()
        for d in range(1, nhead):
            head_share(d).wait_recv()
        total = sq_in[0]
        for d in range(1, nhead):
            total = total + sq_in[d]
        norms[NBACK] = lax.rsqrt(total / float(nhead * dh) + EPSILON)

    def mix(s):
        norm = jnp.concatenate([norms[s, j : j + 1, :] for j in range(rows // 128)], axis=1)

        @pl.loop(0, dh // 32)
        def _(i):
            delta[aligned(i, 32), :] = (mixed_rows(s, i) * norm).astype(BF16)

        product = dot_nt(probs[s], delta[0:dh, :])
        if s == NBACK:
            back[...] = product
        else:
            back[...] = back[...] + product

    load_a.wait()
    gradients(0)
    send_halo(0, 1, 2, 3)
    scatter_z(0, 0)
    send_keys(0, 3)
    scatter_z(0, 1)
    send_keys(3, 6)
    gather_z(0, 0)
    send_keys(6, 9)
    gather_z(0, 1)
    send_keys(9, 12)
    gather_y(0, 0)
    gather_y(0, 1)
    finish_y(0, 0)
    update(0, 0)
    finish_y(0, 1)
    update(0, 1)
    send_keys(12, 15)
    gradients(1)
    for d in range(1, NBACK + 1):
        halo(0, d).wait_recv()
    scatter_z(1, 0)
    send_keys(15, 18)
    scatter_z(1, 1)
    send_keys(18, 21)
    apply_first()
    gather_z(1, 0)
    send_keys(21, 24)
    gather_z(1, 1)
    attend()
    gather_y(1, 0)
    gather_y(1, 1)
    finish_y(1, 0)
    update(1, 0)
    apply_second()
    send_halo(1, 1, 3, 2)
    finish_y(1, 1)
    update(1, 1)
    w2t[1] = weights[2, 2 * hid : 3 * hid, :].T
    project(NBACK)
    share_norm()
    send_halo(2, 1, 3, 2)
    mix(NBACK)
    for d in (1, 3, 2):
        halo(1, d).wait_recv()
        project(NBACK - d)
        halo(2, d).wait_recv()
        mix(NBACK - d)
    out_ref[...] = (back[...] * gain_ref[...].reshape(1, dh)).astype(BF16)
    wait_keys(True)
    for r in range(2):
        for c in range(2):
            for d in range(1, NY):
                y_scatter(r, c, d).wait_send()
                y_gather(r, c, d, y).wait_send()

            @pl.loop(1, nz)
            def _(d):
                z_scatter(r, c, d).wait_send()
                z_gather(r, c, d, z).wait_send()
    for which in range(3):
        for d in range(1, NBACK + 1):
            halo(which, d).wait_send()
    for d in range(1, nhead):
        head_share(d).wait_send()


def shards(queries, keys_fast, values_fast, keys_attn, w_one, w_three, w_two, step_size, norm_gain, group_ids, window_ids):
    rows, dh = queries.shape
    hid = w_one.shape[2]
    nz = lax.axis_size("tok") // NY
    nhead = lax.axis_size("head")
    dma = pltpu.SemaphoreType.DMA
    vmem = pl.BlockSpec(memory_space=pltpu.VMEM)
    anywhere = pl.BlockSpec(memory_space=pl.ANY)

    def chunk(height):
        piece = height // NY * (dh // 128)
        block = piece // nz
        return (
            pltpu.VMEM((2, NY, piece, 128), BF16),
            pltpu.VMEM((2, NY - 1, piece, 128), BF16),
            pltpu.VMEM((piece, 128), F32),
            pltpu.VMEM((2, piece, 128), BF16),
            pltpu.VMEM((block, 128), F32),
            pltpu.VMEM((2, nz - 1, block, 128), BF16),
            pltpu.VMEM((2, NY, piece, 128), BF16),
            dma((2, 2, NY - 1)),
            dma((2, 2, nz - 1)),
            dma((2, 2, nz - 1)),
            dma((2, 2, NY - 1)),
        )

    return pl.pallas_call(
        functools.partial(kernel, (nz, nhead, rows, dh, hid)),
        out_shape=jax.ShapeDtypeStruct((rows, dh), BF16),
        in_specs=[vmem] * 10 + [anywhere],
        out_specs=vmem,
        scratch_shapes=[
            pltpu.VMEM((NBACK + 1, rows, dh), BF16),
            pltpu.VMEM((NBACK + 1, 8, rows), jnp.int32),
            pltpu.VMEM((2 * hid, rows), F32),
            pltpu.VMEM((rows, rows), F32),
            pltpu.VMEM((3 * hid, rows), BF16),
            pltpu.VMEM((3, 3 * hid, dh), BF16),
            pltpu.VMEM((2, dh, hid), BF16),
            pltpu.VMEM((NBACK + 1, rows, rows), F32),
            pltpu.VMEM((NBACK + 1, rows, rows), BF16),
            pltpu.VMEM((hid, rows), BF16),
            pltpu.VMEM((NBACK + 1, hid, rows), BF16),
            pltpu.VMEM((dh, rows), F32),
            pltpu.VMEM((NBACK + 1, rows // 128, 128), F32),
            pltpu.VMEM((nhead, rows // 128, 128), F32),
            dma(()),
            dma((2, 3, NBACK)),
            dma((2, nhead - 1)),
            dma((2, NBACK, KEY_PARTS)),
            chunk(2 * hid),
            chunk(hid),
        ],
        compiler_params=pltpu.CompilerParams(
            collective_id=0, has_side_effects=True, vmem_limit_bytes=56 * 1024 * 1024
        ),
        name="fast_weight_attention",
    )(
        keys_fast,
        values_fast,
        w_one,
        w_three,
        w_two,
        step_size.reshape(1, 1),
        norm_gain,
        group_ids,
        window_ids,
        queries,
        keys_attn,
    )


def solution(mesh):
    in_specs = (
        P("tok", "head"),
        P("tok", "head"),
        P("tok", "head"),
        P("tok", "head"),
        P("head", None, None),
        P("head", None, None),
        P("head", None, None),
        P("head"),
        P("head"),
        P("tok"),
        P("tok"),
    )
    return jax.shard_map(shards, mesh=mesh, in_specs=in_specs, out_specs=P("tok", "head"), check_vma=False)
```

```python
import functools
import math

import jax
import jax.numpy as jnp
from jax import lax
from jax.experimental import pallas as pl
from jax.experimental.pallas import tpu as pltpu
from jax.sharding import PartitionSpec as P

NY = 4
NCORE = 2
NBACK = 3
KEY_PARTS = 8
EPSILON = 1e-06
MESH = pl.DeviceIdType.MESH
F32 = jnp.float32
BF16 = jnp.bfloat16


def dot_nt(a, b):
    return lax.dot_general(a, b, (((1,), (1,)), ((), ())), preferred_element_type=F32)


def dot_nn(a, b):
    return lax.dot_general(a, b, (((1,), (0,)), ((), ())), preferred_element_type=F32)


def sigmoid(x):
    return 0.5 * jnp.tanh(0.5 * x) + 0.5


def aligned(index, step):
    return pl.ds(pl.multiple_of(index * step, step), step)


def kernel(
    dims,
    k_ref,
    v_ref,
    w1_ref,
    w3_ref,
    w2_ref,
    rate_ref,
    gain_ref,
    gid_ref,
    wid_ref,
    q_ref,
    a_hbm,
    out_ref,
    aall,
    ids,
    pre,
    back,
    delta,
    weights,
    w2t,
    scores,
    probs,
    hidden_first,
    hidden,
    fast,
    norms,
    sq_in,
    local_sem,
    halo_sems,
    head_sems,
    key_sems,
    *chunks,
):
    nz, nhead, rows, dh, hid = dims
    ntok = nz * NY
    cols = dh // 128
    t = lax.axis_index("tok")
    h = lax.axis_index("head")
    z = lax.div(t, NY)
    y = lax.rem(t, NY)
    starts = (0, 2 * hid)
    heights = (2 * hid // NY, hid // NY)
    pieces = tuple(height * cols for height in heights)
    blocks = tuple(piece // nz for piece in pieces)

    def y_peer(d):
        return z * NY + lax.rem(y + d, NY)

    def far_first(i):
        half = lax.div(i + 1, 2)
        return nz // 2 + half * (1 - 2 * lax.rem(i, 2))

    def z_peer(d):
        return lax.rem(z + d, nz) * NY + y

    def remote(src, dst, sems, index, **where):
        return pltpu.make_async_remote_copy(
            src_ref=src,
            dst_ref=dst,
            send_sem=sems.at[(0, *index)],
            recv_sem=sems.at[(1, *index)],
            device_id=where,
            device_id_type=MESH,
        )

    load_a = pltpu.make_async_copy(a_hbm, aall.at[NBACK], local_sem)
    load_a.start()

    barrier = pltpu.get_barrier_semaphore()

    def greet(**where):
        pl.semaphore_signal(barrier, inc=1, device_id=where, device_id_type=MESH)

    @pl.loop(1, nz)
    def _(d):
        greet(tok=z_peer(d))

    for d in range(1, NY):
        greet(tok=y_peer(d))
    for d in range(1, NBACK + 1):
        greet(tok=lax.rem(t + ntok - d, ntok))
    for d in range(1, nhead):
        greet(head=lax.rem(h + d, nhead))

    ids[NBACK, 0:1, :] = wid_ref[...].reshape(1, rows)
    ids[NBACK, 1:2, :] = gid_ref[...].reshape(1, rows)
    weights[0, 0:hid, :] = w1_ref[0].T
    weights[0, hid : 2 * hid, :] = w3_ref[0].T
    weights[0, 2 * hid : 3 * hid, :] = w2_ref[0]

    def y_scatter(r, c, d):
        grad_send, y_in, sems = chunks[c][0], chunks[c][1], chunks[c][7]
        return remote(
            grad_send.at[r, lax.rem(y + d, NY)], y_in.at[r, d - 1], sems, (r, d - 1), tok=y_peer(d)
        )

    def z_scatter(r, c, d):
        z_out, z_in, sems = chunks[c][3], chunks[c][5], chunks[c][8]
        n = lax.rem(z + d, nz)
        return remote(
            z_out.at[r, aligned(n, blocks[c])], z_in.at[r, d - 1], sems, (r, d - 1), tok=z_peer(d)
        )

    def z_gather(r, c, d, owner):
        part = chunks[c][6].at[r, y, aligned(owner, blocks[c])]
        return remote(part, part, chunks[c][9], (r, d - 1), tok=z_peer(d))

    def y_gather(r, c, d, owner):
        part = chunks[c][6].at[r, owner]
        return remote(part, part, chunks[c][10], (r, d - 1), tok=y_peer(d))

    def key_piece(n):
        d = (1, 3, 2)[n % NBACK]
        part = n // NBACK
        here = slice(part * rows // KEY_PARTS, (part + 1) * rows // KEY_PARTS)
        return remote(
            aall.at[NBACK, here],
            aall.at[NBACK - d, here],
            key_sems,
            (d - 1, part),
            tok=lax.rem(t + d, ntok),
        )

    def reaches(shard, n):
        left = lax.rem(shard, 3)
        return left != 0 if n // NBACK >= KEY_PARTS // 2 else left == 1

    def send_keys(first, last):
        for n in range(first, last):
            if n % NBACK == 1:

                @pl.when(reaches(lax.rem(t + NBACK, ntok), n))
                def _():
                    key_piece(n).start()
            else:
                key_piece(n).start()

    def wait_keys(sent):
        for n in range(NBACK * KEY_PARTS):
            wait = key_piece(n).wait_send if sent else key_piece(n).wait_recv
            if n % NBACK == 1:
                pl.when(reaches(lax.rem(t + NBACK, ntok) if sent else t, n))(wait)
            else:
                wait()

    def halo(which, d):
        buffer = (ids, hidden, norms)[which]
        return remote(
            buffer.at[NBACK], buffer.at[NBACK - d], halo_sems, (which, d - 1), tok=lax.rem(t + d, ntok)
        )

    def head_share(d):
        return remote(sq_in.at[0], sq_in.at[d], head_sems, (d - 1,), head=lax.rem(h + d, nhead))

    def send_halo(which, *distances):
        for d in distances:
            halo(which, d).start()

    def swiglu(i):
        p1 = pre[aligned(i, 32), :]
        p3 = pre[pl.ds(pl.multiple_of(hid + i * 32, 32), 32), :]
        return p1 * sigmoid(p1) * p3

    def gradients(r):
        pre[...] = dot_nt(weights[r, 0 : 2 * hid, :], k_ref[...])
        back[0:hid, :] = dot_nt(weights[r, 2 * hid : 3 * hid, :], v_ref[...])
        mask = (ids[NBACK, 1:2, :] == r).astype(F32)

        @pl.loop(0, hid // 32)
        def _(i):
            p1 = pre[aligned(i, 32), :]
            p3 = pre[pl.ds(pl.multiple_of(hid + i * 32, 32), 32), :]
            b = back[aligned(i, 32), :] * mask
            s1 = sigmoid(p1)
            silu = p1 * s1
            delta[aligned(i, 32), :] = (-b * p3 * s1 * (1.0 + p1 * (1.0 - s1))).astype(BF16)
            delta[pl.ds(pl.multiple_of(hid + i * 32, 32), 32), :] = (-b * silu).astype(BF16)
            delta[pl.ds(pl.multiple_of(2 * hid + i * 32, 32), 32), :] = (-silu * p3 * mask).astype(BF16)

        if r == 0:
            pl.semaphore_wait(barrier, (NY - 1) + (nz - 1) + NBACK + (nhead - 1))
        for c in range(2):
            grad_send, grad_own = chunks[c][0], chunks[c][2]
            height = heights[c]
            for d in (1, 3, 2, 0):
                p = lax.rem(y + d, NY)
                here = pl.ds(pl.multiple_of(starts[c] + p * height, height), height)
                grad = dot_nn(delta[here, :], (k_ref, v_ref)[c][...])
                for j in range(cols):
                    part = grad[:, j * 128 : (j + 1) * 128]
                    if d:
                        grad_send[r, p, j * height : (j + 1) * height, :] = part.astype(BF16)
                    else:
                        grad_own[j * height : (j + 1) * height, :] = part
                if d:
                    y_scatter(r, c, d).start()

    def scatter_z(r, c):
        y_in, grad_own, z_out, z_own = chunks[c][1:5]
        for d in range(1, NY):
            y_scatter(r, c, d).wait_recv()

        def total(n):
            own = grad_own[aligned(n, blocks[c]), :]
            for d in range(1, NY):
                own = own + y_in[r, d - 1, aligned(n, blocks[c]), :].astype(F32)
            return own

        @pl.loop(0, nz - 1)
        def _(i):
            d = far_first(i)
            z_out[r, aligned(lax.rem(z + d, nz), blocks[c]), :] = total(lax.rem(z + d, nz)).astype(BF16)
            z_scatter(r, c, d).start()

        z_own[...] = total(z)

    def gather_z(r, c):
        z_own, z_in, gathered = chunks[c][4:7]

        def add(d, total):
            z_scatter(r, c, d).wait_recv()
            return total + z_in[r, d - 1].astype(F32)

        total = lax.fori_loop(1, nz, add, z_own[...])
        gathered[r, y, aligned(z, blocks[c]), :] = total.astype(BF16)

        @pl.loop(0, nz - 1)
        def _(i):
            z_gather(r, c, far_first(i), z).start()

    def gather_y(r, c):
        @pl.loop(1, nz)
        def _(d):
            z_gather(r, c, d, lax.rem(z + nz - d, nz)).wait_recv()

        for d in (1, 3, 2):
            y_gather(r, c, d, y).start()

    def finish_y(r, c):
        for d in range(1, NY):
            y_gather(r, c, d, lax.rem(y + NY - d, NY)).wait_recv()

    def step_scale(r, c, owners):
        gathered = chunks[c][6]
        total = jnp.zeros((8, 128), F32)
        for p in owners:
            for j in range(cols):
                x = gathered[r, p, j * heights[c] : (j + 1) * heights[c], :].astype(F32)
                total = total + jnp.sum((x * x).reshape(-1, 8, 128), axis=0)
        mean = jnp.sum(total, axis=(0, 1), keepdims=True) / float(hid * dh)
        return rate_ref[...] * lax.rsqrt(mean + EPSILON)

    def update(r, c):
        gathered = chunks[c][6]
        height = heights[c]
        parts = ((0, 1), (2, 3)) if c == 0 else ((0, 1, 2, 3),)
        for owners in parts:
            scale = step_scale(r, c, owners)
            for p in owners:
                for j in range(cols):
                    here = slice(starts[c] + p * height, starts[c] + (p + 1) * height)
                    lanes = slice(j * 128, (j + 1) * 128)
                    grad = gathered[r, p, j * height : (j + 1) * height, :].astype(F32)
                    weights[r + 1, here, lanes] = (
                        weights[r, here, lanes].astype(F32) - grad * scale
                    ).astype(BF16)

    def attend():
        wait_keys(False)

        @pl.loop(0, NBACK + 1)
        def _(s):
            scores[s] = dot_nt(q_ref[...], aall[s])

        mark = jnp.broadcast_to(ids[NBACK, 0:1, :].astype(F32), (128, rows)).T
        back[0:rows, 0:128] = mark

        @pl.loop(0, rows // 16)
        def _(i):
            here = aligned(i, 16)
            query_mark = back[here, 0:1] - 1.0
            query_at = t * rows + i * 16 + lax.broadcasted_iota(jnp.int32, (16, rows), 0)
            parts = []
            for s in range(NBACK + 1):
                key_at = (t - NBACK + s) * rows + lax.broadcasted_iota(jnp.int32, (16, rows), 1)
                allowed = (
                    (key_at <= query_at) & (key_at >= 0) & (ids[s, 0:1, :].astype(F32) >= query_mark)
                )
                parts.append(jnp.where(allowed, scores[s, here, :] * (1.0 / math.sqrt(dh)), -1e30))
            top = parts[0]
            for part in parts[1:]:
                top = jnp.maximum(top, part)
            top = jnp.max(top, axis=1, keepdims=True)
            parts = [jnp.exp(part - top) for part in parts]
            whole = parts[0]
            for part in parts[1:]:
                whole = whole + part
            inverse = 1.0 / jnp.sum(whole, axis=1, keepdims=True)
            for s in range(NBACK + 1):
                probs[s, here, :] = (parts[s] * inverse).astype(BF16)

    def apply_first():
        w2t[0] = weights[1, 2 * hid : 3 * hid, :].T
        pre[...] = dot_nt(weights[1, 0 : 2 * hid, :], q_ref[...])

        @pl.loop(0, hid // 32)
        def _(i):
            hidden_first[aligned(i, 32), :] = swiglu(i).astype(BF16)

    def apply_second():
        pre[...] = dot_nt(weights[2, 0 : 2 * hid, :], q_ref[...])
        first = ids[NBACK, 1:2, :] == 0

        @pl.loop(0, hid // 32)
        def _(i):
            here = aligned(i, 32)
            own = hidden_first[here, :].astype(F32)
            hidden[NBACK, here, :] = jnp.where(first, own, swiglu(i)).astype(BF16)

    def project(s):
        fast[...] = dot_nn(w2t[0], hidden[s])
        pre[...] = dot_nn(w2t[1], hidden[s])

    def mixed_rows(s, i):
        here = aligned(i, 32)
        return jnp.where(ids[s, 1:2, :] == 0, fast[here, :], pre[here, :])

    def share_norm():
        def add(i, total):
            x = mixed_rows(NBACK, i)
            return total + jnp.sum((x * x).reshape(4, 8, rows), axis=0)

        total = lax.fori_loop(0, dh // 32, add, jnp.zeros((8, rows), F32))
        total = jnp.sum(total, axis=0, keepdims=True)
        for j in range(rows // 128):
            sq_in[0, j : j + 1, :] = total[:, j * 128 : (j + 1) * 128]
        for d in range(1, nhead):
            head_share(d).start()
        for d in range(1, nhead):
            head_share(d).wait_recv()
        total = sq_in[0]
        for d in range(1, nhead):
            total = total + sq_in[d]
        norms[NBACK] = lax.rsqrt(total / float(nhead * dh) + EPSILON)

    def mix(s):
        norm = jnp.concatenate([norms[s, j : j + 1, :] for j in range(rows // 128)], axis=1)

        @pl.loop(0, dh // 32)
        def _(i):
            delta[aligned(i, 32), :] = (mixed_rows(s, i) * norm).astype(BF16)

        product = dot_nt(probs[s], delta[0:dh, :])
        if s == NBACK:
            back[...] = product
        else:
            back[...] = back[...] + product

    load_a.wait()
    gradients(0)
    send_keys(0, 3)
    send_halo(0, 1, 2, 3)
    scatter_z(0, 0)
    send_keys(3, 6)
    scatter_z(0, 1)
    send_keys(6, 9)
    gather_z(0, 0)
    send_keys(9, 12)
    gather_z(0, 1)
    send_keys(12, 15)
    gather_y(0, 0)
    gather_y(0, 1)
    send_keys(15, 18)
    finish_y(0, 0)
    update(0, 0)
    finish_y(0, 1)
    update(0, 1)
    send_keys(18, 21)
    gradients(1)
    for d in range(1, NBACK + 1):
        halo(0, d).wait_recv()
    scatter_z(1, 0)
    send_keys(21, 24)
    scatter_z(1, 1)
    apply_first()
    gather_z(1, 0)
    gather_z(1, 1)
    gather_y(1, 0)
    gather_y(1, 1)
    attend()
    finish_y(1, 0)
    update(1, 0)
    apply_second()
    send_halo(1, 1, 3, 2)
    finish_y(1, 1)
    update(1, 1)
    w2t[1] = weights[2, 2 * hid : 3 * hid, :].T
    project(NBACK)
    share_norm()
    send_halo(2, 1, 3, 2)
    mix(NBACK)
    for d in (1, 3, 2):
        halo(1, d).wait_recv()
        project(NBACK - d)
        halo(2, d).wait_recv()
        mix(NBACK - d)
    out_ref[...] = (back[...] * gain_ref[...].reshape(1, dh)).astype(BF16)

    wait_keys(True)
    for r in range(2):
        for c in range(2):
            for d in range(1, NY):
                y_scatter(r, c, d).wait_send()
                y_gather(r, c, d, y).wait_send()

            @pl.loop(1, nz)
            def _(d):
                z_scatter(r, c, d).wait_send()
                z_gather(r, c, d, z).wait_send()

    for which in range(3):
        for d in range(1, NBACK + 1):
            halo(which, d).wait_send()
    for d in range(1, nhead):
        head_share(d).wait_send()


def shards(queries, keys_fast, values_fast, keys_attn, w_one, w_three, w_two, step_size, norm_gain, group_ids, window_ids):
    rows, dh = queries.shape
    hid = w_one.shape[2]
    nz = lax.axis_size("tok") // NY
    nhead = lax.axis_size("head")
    dma = pltpu.SemaphoreType.DMA
    vmem = pl.BlockSpec(memory_space=pltpu.VMEM)
    anywhere = pl.BlockSpec(memory_space=pl.ANY)

    def chunk(height):
        piece = height // NY * (dh // 128)
        block = piece // nz
        return (
            pltpu.VMEM((2, NY, piece, 128), BF16),
            pltpu.VMEM((2, NY - 1, piece, 128), BF16),
            pltpu.VMEM((piece, 128), F32),
            pltpu.VMEM((2, piece, 128), BF16),
            pltpu.VMEM((block, 128), F32),
            pltpu.VMEM((2, nz - 1, block, 128), BF16),
            pltpu.VMEM((2, NY, piece, 128), BF16),
            dma((2, 2, NY - 1)),
            dma((2, 2, nz - 1)),
            dma((2, 2, nz - 1)),
            dma((2, 2, NY - 1)),
        )

    return pl.pallas_call(
        functools.partial(kernel, (nz, nhead, rows, dh, hid)),
        out_shape=jax.ShapeDtypeStruct((rows, dh), BF16),
        in_specs=[vmem] * 10 + [anywhere],
        out_specs=vmem,
        scratch_shapes=[
            pltpu.VMEM((NBACK + 1, rows, dh), BF16),
            pltpu.VMEM((NBACK + 1, 8, rows), jnp.int32),
            pltpu.VMEM((2 * hid, rows), F32),
            pltpu.VMEM((rows, rows), F32),
            pltpu.VMEM((3 * hid, rows), BF16),
            pltpu.VMEM((3, 3 * hid, dh), BF16),
            pltpu.VMEM((2, dh, hid), BF16),
            pltpu.VMEM((NBACK + 1, rows, rows), F32),
            pltpu.VMEM((NBACK + 1, rows, rows), BF16),
            pltpu.VMEM((hid, rows), BF16),
            pltpu.VMEM((NBACK + 1, hid, rows), BF16),
            pltpu.VMEM((dh, rows), F32),
            pltpu.VMEM((NBACK + 1, rows // 128, 128), F32),
            pltpu.VMEM((nhead, rows // 128, 128), F32),
            dma(()),
            dma((2, 3, NBACK)),
            dma((2, nhead - 1)),
            dma((2, NBACK, KEY_PARTS)),
            chunk(2 * hid),
            chunk(hid),
        ],
        compiler_params=pltpu.CompilerParams(
            collective_id=0, has_side_effects=True, vmem_limit_bytes=56 * 1024 * 1024
        ),
        name="fast_weight_attention",
    )(
        keys_fast,
        values_fast,
        w_one,
        w_three,
        w_two,
        step_size.reshape(1, 1),
        norm_gain,
        group_ids,
        window_ids,
        queries,
        keys_attn,
    )


def solution(mesh):
    in_specs = (
        P("tok", "head"),
        P("tok", "head"),
        P("tok", "head"),
        P("tok", "head"),
        P("head", None, None),
        P("head", None, None),
        P("head", None, None),
        P("head"),
        P("head"),
        P("tok"),
        P("tok"),
    )
    return jax.shard_map(shards, mesh=mesh, in_specs=in_specs, out_specs=P("tok", "head"), check_vma=False)
```

```python
import functools
import math

import jax
import jax.numpy as jnp
from jax import lax
from jax.experimental import pallas as pl
from jax.experimental.pallas import tpu as pltpu
from jax.sharding import PartitionSpec as P

NY = 4
NCORE = 2
NBACK = 3
KEY_PARTS = 8
EPSILON = 1e-06
MESH = pl.DeviceIdType.MESH
F32 = jnp.float32
BF16 = jnp.bfloat16


def dot_nt(a, b):
    return lax.dot_general(a, b, (((1,), (1,)), ((), ())), preferred_element_type=F32)


def dot_nn(a, b):
    return lax.dot_general(a, b, (((1,), (0,)), ((), ())), preferred_element_type=F32)


def sigmoid(x):
    return 0.5 * jnp.tanh(0.5 * x) + 0.5


def aligned(index, step):
    return pl.ds(pl.multiple_of(index * step, step), step)


def kernel(
    dims,
    k_ref,
    v_ref,
    w1_ref,
    w3_ref,
    w2_ref,
    rate_ref,
    gain_ref,
    gid_ref,
    wid_ref,
    q_ref,
    a_hbm,
    out_ref,
    aall,
    ids,
    pre,
    back,
    delta,
    weights,
    w2t,
    scores,
    probs,
    hidden_first,
    hidden,
    fast,
    norms,
    sq_in,
    local_sem,
    halo_sems,
    head_sems,
    key_sems,
    *chunks,
):
    nz, nhead, rows, dh, hid = dims
    ntok = nz * NY
    cols = dh // 128
    t = lax.axis_index("tok")
    h = lax.axis_index("head")
    z = lax.div(t, NY)
    y = lax.rem(t, NY)
    starts = (0, 2 * hid)
    heights = (2 * hid // NY, hid // NY)
    pieces = tuple(height * cols for height in heights)
    blocks = tuple(piece // nz for piece in pieces)

    def y_peer(d):
        return z * NY + lax.rem(y + d, NY)

    def far_first(i):
        half = lax.div(i + 1, 2)
        return nz // 2 + half * (1 - 2 * lax.rem(i, 2))

    def z_peer(d):
        return lax.rem(z + d, nz) * NY + y

    def remote(src, dst, sems, index, **where):
        return pltpu.make_async_remote_copy(
            src_ref=src,
            dst_ref=dst,
            send_sem=sems.at[(0, *index)],
            recv_sem=sems.at[(1, *index)],
            device_id=where,
            device_id_type=MESH,
        )

    load_a = pltpu.make_async_copy(a_hbm, aall.at[NBACK], local_sem)
    load_a.start()

    barrier = pltpu.get_barrier_semaphore()

    def greet(**where):
        pl.semaphore_signal(barrier, inc=1, device_id=where, device_id_type=MESH)

    @pl.loop(1, nz)
    def _(d):
        greet(tok=z_peer(d))

    for d in range(1, NY):
        greet(tok=y_peer(d))
    for d in range(1, NBACK + 1):
        greet(tok=lax.rem(t + ntok - d, ntok))
    for d in range(1, nhead):
        greet(head=lax.rem(h + d, nhead))

    ids[NBACK, 0:1, :] = wid_ref[...].reshape(1, rows)
    ids[NBACK, 1:2, :] = gid_ref[...].reshape(1, rows)
    weights[0, 0:hid, :] = w1_ref[0].T
    weights[0, hid : 2 * hid, :] = w3_ref[0].T
    weights[0, 2 * hid : 3 * hid, :] = w2_ref[0]

    def y_scatter(r, c, d):
        grad_send, y_in, sems = chunks[c][0], chunks[c][1], chunks[c][7]
        return remote(
            grad_send.at[r, lax.rem(y + d, NY)], y_in.at[r, d - 1], sems, (r, d - 1), tok=y_peer(d)
        )

    def z_scatter(r, c, d):
        z_out, z_in, sems = chunks[c][3], chunks[c][5], chunks[c][8]
        n = lax.rem(z + d, nz)
        return remote(
            z_out.at[r, aligned(n, blocks[c])], z_in.at[r, d - 1], sems, (r, d - 1), tok=z_peer(d)
        )

    def z_gather(r, c, d, owner):
        part = chunks[c][6].at[r, y, aligned(owner, blocks[c])]
        return remote(part, part, chunks[c][9], (r, d - 1), tok=z_peer(d))

    def y_gather(r, c, d, owner):
        part = chunks[c][6].at[r, owner]
        return remote(part, part, chunks[c][10], (r, d - 1), tok=y_peer(d))

    def key_piece(n):
        d = (1, 3, 2)[n % NBACK]
        part = n // NBACK
        here = slice(part * rows // KEY_PARTS, (part + 1) * rows // KEY_PARTS)
        return remote(
            aall.at[NBACK, here],
            aall.at[NBACK - d, here],
            key_sems,
            (d - 1, part),
            tok=lax.rem(t + d, ntok),
        )

    def reaches(shard, n):
        left = lax.rem(shard, 3)
        return left != 0 if n // NBACK >= KEY_PARTS // 2 else left == 1

    def send_keys(first, last):
        for n in range(first, last):
            if n % NBACK == 1:

                @pl.when(reaches(lax.rem(t + NBACK, ntok), n))
                def _():
                    key_piece(n).start()
            else:
                key_piece(n).start()

    def wait_keys(sent):
        for n in range(NBACK * KEY_PARTS):
            wait = key_piece(n).wait_send if sent else key_piece(n).wait_recv
            if n % NBACK == 1:
                pl.when(reaches(lax.rem(t + NBACK, ntok) if sent else t, n))(wait)
            else:
                wait()

    def halo(which, d):
        buffer = (ids, hidden, norms)[which]
        return remote(
            buffer.at[NBACK], buffer.at[NBACK - d], halo_sems, (which, d - 1), tok=lax.rem(t + d, ntok)
        )

    def head_share(d):
        return remote(sq_in.at[0], sq_in.at[d], head_sems, (d - 1,), head=lax.rem(h + d, nhead))

    def send_halo(which, *distances):
        for d in distances:
            halo(which, d).start()

    def swiglu(i):
        p1 = pre[aligned(i, 32), :]
        p3 = pre[pl.ds(pl.multiple_of(hid + i * 32, 32), 32), :]
        return p1 * sigmoid(p1) * p3

    def gradients(r):
        pre[...] = dot_nt(weights[r, 0 : 2 * hid, :], k_ref[...])
        back[0:hid, :] = dot_nt(weights[r, 2 * hid : 3 * hid, :], v_ref[...])
        mask = (ids[NBACK, 1:2, :] == r).astype(F32)

        @pl.loop(0, hid // 32)
        def _(i):
            p1 = pre[aligned(i, 32), :]
            p3 = pre[pl.ds(pl.multiple_of(hid + i * 32, 32), 32), :]
            b = back[aligned(i, 32), :] * mask
            s1 = sigmoid(p1)
            silu = p1 * s1
            delta[aligned(i, 32), :] = (-b * p3 * s1 * (1.0 + p1 * (1.0 - s1))).astype(BF16)
            delta[pl.ds(pl.multiple_of(hid + i * 32, 32), 32), :] = (-b * silu).astype(BF16)
            delta[pl.ds(pl.multiple_of(2 * hid + i * 32, 32), 32), :] = (-silu * p3 * mask).astype(BF16)

        if r == 0:
            pl.semaphore_wait(barrier, (NY - 1) + (nz - 1) + NBACK + (nhead - 1))
        for c in range(2):
            grad_send, grad_own = chunks[c][0], chunks[c][2]
            height = heights[c]
            for d in (2, 1, 3, 0):
                p = lax.rem(y + d, NY)
                here = pl.ds(pl.multiple_of(starts[c] + p * height, height), height)
                grad = dot_nn(delta[here, :], (k_ref, v_ref)[c][...])
                for j in range(cols):
                    part = grad[:, j * 128 : (j + 1) * 128]
                    if d:
                        grad_send[r, p, j * height : (j + 1) * height, :] = part.astype(BF16)
                    else:
                        grad_own[j * height : (j + 1) * height, :] = part
                if d:
                    y_scatter(r, c, d).start()

    def scatter_z(r, c):
        y_in, grad_own, z_out, z_own = chunks[c][1:5]
        for d in range(1, NY):
            y_scatter(r, c, d).wait_recv()

        def total(n):
            own = grad_own[aligned(n, blocks[c]), :]
            for d in range(1, NY):
                own = own + y_in[r, d - 1, aligned(n, blocks[c]), :].astype(F32)
            return own

        @pl.loop(0, nz - 1)
        def _(i):
            d = far_first(i)
            z_out[r, aligned(lax.rem(z + d, nz), blocks[c]), :] = total(lax.rem(z + d, nz)).astype(BF16)
            z_scatter(r, c, d).start()

        z_own[...] = total(z)

    def gather_z(r, c):
        z_own, z_in, gathered = chunks[c][4:7]

        def add(d, total):
            z_scatter(r, c, d).wait_recv()
            return total + z_in[r, d - 1].astype(F32)

        total = lax.fori_loop(1, nz, add, z_own[...])
        gathered[r, y, aligned(z, blocks[c]), :] = total.astype(BF16)

        @pl.loop(0, nz - 1)
        def _(i):
            z_gather(r, c, far_first(i), z).start()

    def gather_y(r, c):
        @pl.loop(1, nz)
        def _(d):
            z_gather(r, c, d, lax.rem(z + nz - d, nz)).wait_recv()

        for d in (2, 1, 3):
            y_gather(r, c, d, y).start()

    def finish_y(r, c):
        for d in range(1, NY):
            y_gather(r, c, d, lax.rem(y + NY - d, NY)).wait_recv()

    def step_scale(r, c, owners):
        gathered = chunks[c][6]
        total = jnp.zeros((8, 128), F32)
        for p in owners:
            for j in range(cols):
                x = gathered[r, p, j * heights[c] : (j + 1) * heights[c], :].astype(F32)
                total = total + jnp.sum((x * x).reshape(-1, 8, 128), axis=0)
        mean = jnp.sum(total, axis=(0, 1), keepdims=True) / float(hid * dh)
        return rate_ref[...] * lax.rsqrt(mean + EPSILON)

    def update(r, c):
        gathered = chunks[c][6]
        height = heights[c]
        parts = ((0, 1), (2, 3)) if c == 0 else ((0, 1, 2, 3),)
        for owners in parts:
            scale = step_scale(r, c, owners)
            for p in owners:
                for j in range(cols):
                    here = slice(starts[c] + p * height, starts[c] + (p + 1) * height)
                    lanes = slice(j * 128, (j + 1) * 128)
                    grad = gathered[r, p, j * height : (j + 1) * height, :].astype(F32)
                    weights[r + 1, here, lanes] = (
                        weights[r, here, lanes].astype(F32) - grad * scale
                    ).astype(BF16)

    def attend():
        wait_keys(False)

        @pl.loop(0, NBACK + 1)
        def _(s):
            scores[s] = dot_nt(q_ref[...], aall[s])

        mark = jnp.broadcast_to(ids[NBACK, 0:1, :].astype(F32), (128, rows)).T
        back[0:rows, 0:128] = mark

        @pl.loop(0, rows // 16)
        def _(i):
            here = aligned(i, 16)
            query_mark = back[here, 0:1] - 1.0
            query_at = t * rows + i * 16 + lax.broadcasted_iota(jnp.int32, (16, rows), 0)
            parts = []
            for s in range(NBACK + 1):
                key_at = (t - NBACK + s) * rows + lax.broadcasted_iota(jnp.int32, (16, rows), 1)
                allowed = (
                    (key_at <= query_at) & (key_at >= 0) & (ids[s, 0:1, :].astype(F32) >= query_mark)
                )
                parts.append(jnp.where(allowed, scores[s, here, :] * (1.0 / math.sqrt(dh)), -1e30))
            top = parts[0]
            for part in parts[1:]:
                top = jnp.maximum(top, part)
            top = jnp.max(top, axis=1, keepdims=True)
            parts = [jnp.exp(part - top) for part in parts]
            whole = parts[0]
            for part in parts[1:]:
                whole = whole + part
            inverse = 1.0 / jnp.sum(whole, axis=1, keepdims=True)
            for s in range(NBACK + 1):
                probs[s, here, :] = (parts[s] * inverse).astype(BF16)

    def apply_first():
        w2t[0] = weights[1, 2 * hid : 3 * hid, :].T
        pre[...] = dot_nt(weights[1, 0 : 2 * hid, :], q_ref[...])

        @pl.loop(0, hid // 32)
        def _(i):
            hidden_first[aligned(i, 32), :] = swiglu(i).astype(BF16)

    def apply_second():
        pre[...] = dot_nt(weights[2, 0 : 2 * hid, :], q_ref[...])
        first = ids[NBACK, 1:2, :] == 0

        @pl.loop(0, hid // 32)
        def _(i):
            here = aligned(i, 32)
            own = hidden_first[here, :].astype(F32)
            hidden[NBACK, here, :] = jnp.where(first, own, swiglu(i)).astype(BF16)

    def project(s):
        fast[...] = dot_nn(w2t[0], hidden[s])
        pre[...] = dot_nn(w2t[1], hidden[s])

    def mixed_rows(s, i):
        here = aligned(i, 32)
        return jnp.where(ids[s, 1:2, :] == 0, fast[here, :], pre[here, :])

    def share_norm():
        def add(i, total):
            x = mixed_rows(NBACK, i)
            return total + jnp.sum((x * x).reshape(4, 8, rows), axis=0)

        total = lax.fori_loop(0, dh // 32, add, jnp.zeros((8, rows), F32))
        total = jnp.sum(total, axis=0, keepdims=True)
        for j in range(rows // 128):
            sq_in[0, j : j + 1, :] = total[:, j * 128 : (j + 1) * 128]
        for d in range(1, nhead):
            head_share(d).start()
        for d in range(1, nhead):
            head_share(d).wait_recv()
        total = sq_in[0]
        for d in range(1, nhead):
            total = total + sq_in[d]
        norms[NBACK] = lax.rsqrt(total / float(nhead * dh) + EPSILON)

    def mix(s):
        norm = jnp.concatenate([norms[s, j : j + 1, :] for j in range(rows // 128)], axis=1)

        @pl.loop(0, dh // 32)
        def _(i):
            delta[aligned(i, 32), :] = (mixed_rows(s, i) * norm).astype(BF16)

        product = dot_nt(probs[s], delta[0:dh, :])
        if s == NBACK:
            back[...] = product
        else:
            back[...] = back[...] + product

    load_a.wait()
    gradients(0)
    send_keys(0, 3)
    send_halo(0, 1, 2, 3)
    scatter_z(0, 0)
    send_keys(3, 6)
    scatter_z(0, 1)
    send_keys(6, 9)
    gather_z(0, 0)
    send_keys(9, 12)
    gather_z(0, 1)
    send_keys(12, 15)
    gather_y(0, 0)
    gather_y(0, 1)
    send_keys(15, 18)
    finish_y(0, 0)
    update(0, 0)
    finish_y(0, 1)
    update(0, 1)
    send_keys(18, 21)
    gradients(1)
    for d in range(1, NBACK + 1):
        halo(0, d).wait_recv()
    scatter_z(1, 0)
    send_keys(21, 24)
    scatter_z(1, 1)
    apply_first()
    gather_z(1, 0)
    gather_z(1, 1)
    gather_y(1, 0)
    gather_y(1, 1)
    attend()
    finish_y(1, 0)
    update(1, 0)
    apply_second()
    send_halo(1, 2, 1, 3)
    finish_y(1, 1)
    update(1, 1)
    w2t[1] = weights[2, 2 * hid : 3 * hid, :].T
    project(NBACK)
    share_norm()
    send_halo(2, 1, 3, 2)
    mix(NBACK)
    for d in (1, 3, 2):
        halo(1, d).wait_recv()
        project(NBACK - d)
        halo(2, d).wait_recv()
        mix(NBACK - d)
    out_ref[...] = (back[...] * gain_ref[...].reshape(1, dh)).astype(BF16)

    wait_keys(True)
    for r in range(2):
        for c in range(2):
            for d in range(1, NY):
                y_scatter(r, c, d).wait_send()
                y_gather(r, c, d, y).wait_send()

            @pl.loop(1, nz)
            def _(d):
                z_scatter(r, c, d).wait_send()
                z_gather(r, c, d, z).wait_send()

    for which in range(3):
        for d in range(1, NBACK + 1):
            halo(which, d).wait_send()
    for d in range(1, nhead):
        head_share(d).wait_send()


def shards(queries, keys_fast, values_fast, keys_attn, w_one, w_three, w_two, step_size, norm_gain, group_ids, window_ids):
    rows, dh = queries.shape
    hid = w_one.shape[2]
    nz = lax.axis_size("tok") // NY
    nhead = lax.axis_size("head")
    dma = pltpu.SemaphoreType.DMA
    vmem = pl.BlockSpec(memory_space=pltpu.VMEM)
    anywhere = pl.BlockSpec(memory_space=pl.ANY)

    def chunk(height):
        piece = height // NY * (dh // 128)
        block = piece // nz
        return (
            pltpu.VMEM((2, NY, piece, 128), BF16),
            pltpu.VMEM((2, NY - 1, piece, 128), BF16),
            pltpu.VMEM((piece, 128), F32),
            pltpu.VMEM((2, piece, 128), BF16),
            pltpu.VMEM((block, 128), F32),
            pltpu.VMEM((2, nz - 1, block, 128), BF16),
            pltpu.VMEM((2, NY, piece, 128), BF16),
            dma((2, 2, NY - 1)),
            dma((2, 2, nz - 1)),
            dma((2, 2, nz - 1)),
            dma((2, 2, NY - 1)),
        )

    return pl.pallas_call(
        functools.partial(kernel, (nz, nhead, rows, dh, hid)),
        out_shape=jax.ShapeDtypeStruct((rows, dh), BF16),
        in_specs=[vmem] * 10 + [anywhere],
        out_specs=vmem,
        scratch_shapes=[
            pltpu.VMEM((NBACK + 1, rows, dh), BF16),
            pltpu.VMEM((NBACK + 1, 8, rows), jnp.int32),
            pltpu.VMEM((2 * hid, rows), F32),
            pltpu.VMEM((rows, rows), F32),
            pltpu.VMEM((3 * hid, rows), BF16),
            pltpu.VMEM((3, 3 * hid, dh), BF16),
            pltpu.VMEM((2, dh, hid), BF16),
            pltpu.VMEM((NBACK + 1, rows, rows), F32),
            pltpu.VMEM((NBACK + 1, rows, rows), BF16),
            pltpu.VMEM((hid, rows), BF16),
            pltpu.VMEM((NBACK + 1, hid, rows), BF16),
            pltpu.VMEM((dh, rows), F32),
            pltpu.VMEM((NBACK + 1, rows // 128, 128), F32),
            pltpu.VMEM((nhead, rows // 128, 128), F32),
            dma(()),
            dma((2, 3, NBACK)),
            dma((2, nhead - 1)),
            dma((2, NBACK, KEY_PARTS)),
            chunk(2 * hid),
            chunk(hid),
        ],
        compiler_params=pltpu.CompilerParams(
            collective_id=0, has_side_effects=True, vmem_limit_bytes=56 * 1024 * 1024
        ),
        name="fast_weight_attention",
    )(
        keys_fast,
        values_fast,
        w_one,
        w_three,
        w_two,
        step_size.reshape(1, 1),
        norm_gain,
        group_ids,
        window_ids,
        queries,
        keys_attn,
    )


def solution(mesh):
    in_specs = (
        P("tok", "head"),
        P("tok", "head"),
        P("tok", "head"),
        P("tok", "head"),
        P("head", None, None),
        P("head", None, None),
        P("head", None, None),
        P("head"),
        P("head"),
        P("tok"),
        P("tok"),
    )
    return jax.shard_map(shards, mesh=mesh, in_specs=in_specs, out_specs=P("tok", "head"), check_vma=False)
```
